128 devices in a mesh: row: 8 (over z, core), col: 8 (over x, y_lo), dp: 2 (over y_hi).
Axes of the slice: x: 4, y: 4 (y_hi: 2, y_lo: 2; y = y_hi * 2 + y_lo), z: 4, core: 2. Of those that a mesh axis runs over, the one named last changes fastest.
Arguments:
- inputs: bfloat16 [512, 12288], P(('col', 'dp'), 'row'), may hold values from -6 to 6
- out_grad: bfloat16 [512, 12288], P(('col', 'dp'), 'row'), may hold values from -6 to 6
- w_in: bfloat16 [12288, 24576], P('row', ('col', 'dp')), may hold values from -0.0546875 to 0.0546875
- bias_in: float32 [24576], P(('col', 'dp')), may hold values from -4 to 4
- w_out: bfloat16 [24576, 12288], P(('col', 'dp'), 'row'), may hold values from -0.0390625 to 0.0390625
Outputs:
- grad_inputs: bfloat16 [512, 12288], P(('col', 'dp'), 'row')
- grad_w_in: bfloat16 [12288, 24576], P('row', ('col', 'dp'))
- grad_bias: bfloat16 [24576], P(('col', 'dp'))
- grad_w_out: bfloat16 [24576, 12288], P(('col', 'dp'), 'row')
The draws below stay inside these ranges and needn't reach their ends.
All inputs are finite; a program needn't handle non-finite values.
Results may differ from the reference program's by a relative error of at most 0.006.
Values may be sent and summed in bfloat16 or wider, within the bound.
No kernel may reach another device: no remote copies, remote signals or barrier semaphores. Data moves between devices by JAX's collectives and lax.ppermute only.
A program may use at most 128 MiB of HBM per device.

```python
import jax
import jax.numpy as jnp
from jax import lax

D = 12288
FW = 24576
TOKENS = 512


def steps_of(own_key, extent, shards, low, top_value):
    def one(dim, shards_of):
        draws = jax.random.uniform(jax.random.fold_in(jax.random.fold_in(own_key, 6), dim), (shards_of,), jnp.float32, low / len(shards), top_value / len(shards))
        return jnp.repeat(jnp.exp(draws), extent[dim] // shards_of).reshape((-1,) + (1,) * (len(extent) - dim - 1))

    loudness = one(*shards[0])
    for cut in shards[1:]:
        loudness = loudness * one(*cut)
    return loudness


def noise(rng, dims, deviation, limit, shards=(), dtype=jnp.bfloat16):
    loudness = steps_of(rng, dims, shards, -0.22, 0.18) if shards else 1.0
    result = jax.random.normal(rng, dims, jnp.float32) * deviation * loudness
    return jnp.minimum(jnp.maximum(result, -limit), limit).astype(dtype)


def setup_inputs(seed: int = 0) -> dict:
    arg_keys = jax.random.split(jax.random.key(seed), 6)
    return {
        "inputs": noise(arg_keys[0], (TOKENS, D), 1.0, 6.0, ((0, 16), (1, 8))),
        "out_grad": noise(arg_keys[1], (TOKENS, D), 1.0, 6.0, ((0, 16), (1, 8))),
        "w_in": noise(arg_keys[2], (D, FW), D ** -0.5, 0.0546875, ((0, 8), (1, 16))),
        "bias_in": noise(arg_keys[3], (FW,), 1.0, 4.0, ((0, 16),), jnp.float32),
        "w_out": noise(arg_keys[4], (FW, D), FW ** -0.5, 0.0390625, ((0, 16), (1, 8))),
    }


def gelu_tanh(v):
    return jax.nn.gelu(v, approximate=True)

def reference(inputs, out_grad, w_in, bias_in, w_out):
    pre = jnp.dot(inputs, w_in, preferred_element_type=jnp.float32) + bias_in[None, :]
    activated = gelu_tanh(pre).astype(jnp.bfloat16)
    act_grad = jnp.dot(out_grad, w_out.T, preferred_element_type=jnp.float32)
    _, pullback = jax.vjp(gelu_tanh, pre)
    pre_grad = pullback(act_grad)[0].astype(jnp.bfloat16)
    grad_w_out = jnp.dot(activated.T, out_grad, preferred_element_type=jnp.float32).astype(jnp.bfloat16)
    grad_w_in = jnp.dot(inputs.T, pre_grad, preferred_element_type=jnp.float32).astype(jnp.bfloat16)
    grad_bias = lax.optimization_barrier(jnp.sum(pre_grad.astype(jnp.float32), axis=0)).astype(jnp.bfloat16)
    grad_inputs = jnp.dot(pre_grad, w_in.T, preferred_element_type=jnp.float32).astype(jnp.bfloat16)
    return (grad_inputs, grad_w_in, grad_bias, grad_w_out)
```

```python
import jax
import jax.numpy as jnp
from jax import lax
from jax.sharding import PartitionSpec as P

AXES = ("row", "col", "dp")
Z, CORES, X, Y = 4, 2, 4, 4


def place(z, core, x, y):
    return ((z * CORES + core) * 8 + x * 2 + y % 2) * 2 + y // 2


def pairs(source):
    every = [(z, c, x, y) for z in range(Z) for c in range(CORES) for x in range(X) for y in range(Y)]
    return [(place(*source(*at)), place(*at)) for at in every]


def along_first(step):
    return pairs(lambda z, c, x, y: (z, c, x, (y + step) % Y) if c else (z, c, (x + step) % X, y))


def along_second(step):
    return pairs(lambda z, c, x, y: (z, c, (x + step) % X, y) if c else (z, c, x, (y + step) % Y))


def along_z(step):
    return pairs(lambda z, c, x, y: ((z + step) % Z, c, x, y))


OTHER_CORE = pairs(lambda z, c, x, y: (z, 1 - c, x, y))


def send(value, perm):
    return lax.ppermute(value, AXES, perm)


def gelu_tanh(value):
    return jax.nn.gelu(value, approximate=True)


def activate(pre, act_grad):
    activated = gelu_tanh(pre).astype(jnp.bfloat16)
    _, pullback = jax.vjp(gelu_tanh, pre)
    return activated, pullback(act_grad)[0].astype(jnp.bfloat16)


def swap_order(value):
    tokens = value.shape[-2]
    lead = value.shape[:-2]
    blocks = value.reshape(lead + (4, 4, tokens // 16, value.shape[-1]))
    return jnp.swapaxes(blocks, -4, -3).reshape(value.shape)


def body(inputs, out_grad, w_in, bias_in, w_out):
    bf16, f32 = jnp.bfloat16, jnp.float32
    tokens, features = inputs.shape
    hidden = w_in.shape[1]
    half = hidden // 2
    row = lax.axis_index("row")
    z, core = row // CORES, row % CORES

    mine = jnp.stack([inputs, out_grad])
    line = jnp.concatenate([mine] + [send(mine, along_first(d)) for d in (1, 2, 3)], axis=1)
    plane = jnp.concatenate([line] + [send(line, along_second(d)) for d in (1, 2, 3)], axis=1)
    every_in, every_grad = plane[0], plane[1]

    forward_term = jnp.dot(every_in, w_in, preferred_element_type=f32).astype(bf16)
    backward_term = lax.dot_general(
        every_grad, w_out, (((1,), (1,)), ((), ())), preferred_element_type=f32
    ).astype(bf16)
    terms = jnp.stack([forward_term, backward_term])
    keep = lax.dynamic_slice_in_dim(terms, core * half, half, 2)
    give = lax.dynamic_slice_in_dim(terms, (1 - core) * half, half, 2)
    chip = keep.astype(f32) + swap_order(send(give, OTHER_CORE)).astype(f32)
    chip = chip.reshape(2, Z, 4 * tokens, half)
    chip16 = chip.astype(bf16)
    total = lax.dynamic_index_in_dim(chip, z, 1, keepdims=False)
    for d in (1, 2, 3):
        part = lax.dynamic_index_in_dim(chip16, (z - d) % Z, 1, keepdims=False)
        total = total + send(part, along_z(d)).astype(f32)

    bias = lax.dynamic_slice_in_dim(bias_in, core * half, half, 0)
    both = jnp.stack(activate(total[0] + bias[None, :], total[1]))

    gathered = jnp.stack([both] + [send(both, along_z(d)) for d in (1, 2, 3)], axis=1)
    mine_half = jnp.roll(gathered, z, axis=1).reshape(2, 16 * tokens, half)
    other_half = swap_order(send(mine_half, OTHER_CORE))
    hidden_all = jnp.where(
        core == 0,
        jnp.concatenate([mine_half, other_half], axis=2),
        jnp.concatenate([other_half, mine_half], axis=2),
    )
    activ_all, pre_grad_all = hidden_all[0], hidden_all[1]

    share = lax.dot_general(
        pre_grad_all, w_in, (((1,), (1,)), ((), ())), preferred_element_type=f32
    ).astype(bf16)
    share = share.reshape(4, 4 * tokens, features)
    line_sum = share[0].astype(f32)
    for b in (1, 2, 3):
        line_sum = line_sum + send(share[b], along_second(4 - b)).astype(f32)
    line_sum = line_sum.reshape(4, tokens, features)
    line16 = line_sum.astype(bf16)
    grad_inputs = line_sum[0]
    for a in (1, 2, 3):
        grad_inputs = grad_inputs + send(line16[a], along_first(4 - a)).astype(f32)
    grad_inputs = grad_inputs.astype(bf16)

    grad_w_out = lax.dot_general(
        activ_all, every_grad, (((0,), (0,)), ((), ())), preferred_element_type=f32
    ).astype(bf16)
    grad_w_in = lax.dot_general(
        every_in, pre_grad_all, (((0,), (0,)), ((), ())), preferred_element_type=f32
    ).astype(bf16)
    grad_bias = jnp.sum(pre_grad_all, axis=0, dtype=f32).astype(bf16)
    return (grad_inputs, grad_w_in, grad_bias, grad_w_out)


def solution(mesh):
    in_specs = (
        P(("col", "dp"), "row"),
        P(("col", "dp"), "row"),
        P("row", ("col", "dp")),
        P(("col", "dp")),
        P(("col", "dp"), "row"),
    )
    out_specs = (
        P(("col", "dp"), "row"),
        P("row", ("col", "dp")),
        P(("col", "dp")),
        P(("col", "dp"), "row"),
    )
    return jax.shard_map(body, mesh=mesh, in_specs=in_specs, out_specs=out_specs, check_vma=False)
```

```python
import functools

import jax
import jax.numpy as jnp
from jax import lax
from jax.experimental import pallas as pl
from jax.experimental.pallas import tpu as pltpu
from jax.sharding import PartitionSpec as P

AXES = ("row", "col", "dp")
Z, CORES, X, Y = 4, 2, 4, 4
BF16, F32 = jnp.bfloat16, jnp.float32
SIGN = -1
TILE = 256
MIB = 1 << 20


def place(z, core, x, y):
    return ((z * CORES + core) * 8 + x * 2 + y % 2) * 2 + y // 2


def pairs(source):
    every = [(z, c, x, y) for z in range(Z) for c in range(CORES) for x in range(X) for y in range(Y)]
    return [(place(*source(*at)), place(*at)) for at in every]


def along_first(step):
    step = SIGN * step
    return pairs(lambda z, c, x, y: (z, c, x, (y + step) % Y) if c else (z, c, (x + step) % X, y))


def along_second(step):
    step = SIGN * step
    return pairs(lambda z, c, x, y: (z, c, (x + step) % X, y) if c else (z, c, x, (y + step) % Y))


Z_ONE = pairs(lambda z, c, x, y: (z ^ (3 if c else 1), c, x, y))
Z_TWO = pairs(lambda z, c, x, y: (z ^ (1 if c else 3), c, x, y))
OTHER_CORE = pairs(lambda z, c, x, y: (z, 1 - c, x, y))


def send(value, perm):
    return lax.ppermute(value, AXES, perm)


def ring(value, along):
    return [send(value, along(d)) for d in (3, 2, 1)][::-1]


def local(kernel, outs, args, limit=8, flops=0, follow=(), result=pltpu.VMEM):
    spec = pl.BlockSpec(memory_space=pltpu.VMEM)
    count = len(args)

    def run(*refs):
        kernel(*refs[:count], *refs[count + len(follow) :])

    args = [pltpu.with_memory_space_constraint(a, pltpu.VMEM) for a in args]
    moved = sum(a.size * a.dtype.itemsize for a in args)
    return pl.pallas_call(
        run,
        out_shape=[result(shape, dtype) for shape, dtype in outs],
        in_specs=[spec] * count + [pl.BlockSpec(memory_space=pltpu.HBM if f.size > 2**20 else pl.ANY) for f in follow],
        out_specs=[spec] * len(outs),
        compiler_params=pltpu.CompilerParams(vmem_limit_bytes=limit * MIB),
        cost_estimate=pl.CostEstimate(flops=0, bytes_accessed=0, transcendentals=0),
    )(*args, *follow)


def at():
    row = lax.axis_index("row")
    z, core = row >> 1, row & 1
    return z, core, z ^ (1 + 2 * core), z ^ (3 - 2 * core)


def span(index, size):
    return pl.ds(pl.multiple_of(index * size, size), size)


def swapped_rows(ref, block, tokens):
    return jnp.concatenate([ref[span(a * 4 + block, tokens), :] for a in range(4)], axis=0)


def line_kernel(last, far, near, mine, ins, grads):
    tokens = mine.shape[1]
    for i, ref in enumerate((mine, near, far, last)):
        ins[i * tokens : (i + 1) * tokens, :] = ref[0]
        grads[i * tokens : (i + 1) * tokens, :] = ref[1]


def product_kernel(transposed, halves, d, c, b, a, weight, *outs):
    core = lax.axis_index("row") & 1
    rows = jnp.concatenate([a[...], b[...], c[...], d[...]], axis=0)
    for half, out in zip(halves, outs):
        tiles = out.shape[1] // TILE
        for n in range(tiles):
            part = span((core ^ half) * tiles + n, TILE)
            if transposed:
                value = lax.dot_general(
                    rows, weight[part, :], (((1,), (1,)), ((), ())), preferred_element_type=F32
                )
            else:
                value = jnp.dot(rows, weight[:, part], preferred_element_type=F32)
            out[:, n * TILE : (n + 1) * TILE] = value.astype(out.dtype)


def first_sum_kernel(keep, got, sent, mine, near):
    z, _, one, two = at()
    size = mine.shape[0]

    def block(index):
        return keep[span(index, size), :] + swapped_rows(got, index, size // 4).astype(F32)

    sent[0] = block(one).astype(BF16)
    sent[1] = block(z ^ 2).astype(BF16)
    near[...] = block(two)
    mine[...] = block(z)


def second_sum_kernel(pre, pre_near, pre_got, act, act_near, act_got, sent, pre_out, act_out):
    sent[0] = (pre_near[...] + pre_got[1].astype(F32)).astype(BF16)
    sent[1] = (act_near[...] + act_got[1].astype(F32)).astype(BF16)
    pre_out[...] = pre[...] + pre_got[0].astype(F32)
    act_out[...] = act[...] + act_got[0].astype(F32)


def gelu_parts(value):
    scale = 0.7978845608028654
    inner = jnp.tanh(scale * (value + 0.044715 * value * value * value))
    slope = 0.5 * (1.0 + inner) + 0.5 * value * (1.0 - inner * inner) * (
        scale * (1.0 + 3.0 * 0.044715 * value * value)
    )
    return 0.5 * value * (1.0 + inner), slope


def activate_kernel(pre, act, got, bias, activated, pre_grad):
    core = lax.axis_index("row") & 1
    value = pre[...] + got[0].astype(F32) + bias[:, span(core, pre.shape[1])]
    result, slope = gelu_parts(value)
    activated[...] = result.astype(BF16)
    pre_grad[...] = ((act[...] + got[1].astype(F32)) * slope).astype(BF16)


def pair_kernel(own, near, out):
    out[0] = own[...]
    out[1] = near[...]


def place_kernel(own, near, far, out):
    z, _, one, two = at()
    size = own.shape[0]
    out[span(z, size), :] = own[...]
    out[span(two, size), :] = near[...]
    out[span(one, size), :] = far[0]
    out[span(z ^ 2, size), :] = far[1]


def join(mine, other, out):
    core = lax.axis_index("row") & 1
    tokens, half = mine.shape[0] // 16, mine.shape[1]
    out[:, span(core, half)] = mine[...]
    for b in range(4):
        out[b * 4 * tokens : (b + 1) * 4 * tokens, span(1 - core, half)] = swapped_rows(other, b, tokens)


def share_own_kernel(mine, weight, out):
    core = lax.axis_index("row") & 1
    for n in range(out.shape[1] // TILE):
        tile = slice(n * TILE, (n + 1) * TILE)
        out[:, tile] = lax.dot_general(
            mine[...],
            weight[tile, span(core, mine.shape[1])],
            (((1,), (1,)), ((), ())),
            preferred_element_type=F32,
        )


def share_other_kernel(partial, other, weight, *outs):
    core = lax.axis_index("row") & 1
    size = outs[0].shape[0]
    rows = jnp.concatenate([swapped_rows(other, b, size // 4) for b in range(4)], axis=0)
    for n in range(partial.shape[1] // TILE):
        tile = slice(n * TILE, (n + 1) * TILE)
        value = partial[:, tile] + lax.dot_general(
            rows,
            weight[tile, span(1 - core, other.shape[1])],
            (((1,), (1,)), ((), ())),
            preferred_element_type=F32,
        )
        for b, out in enumerate(outs):
            out[:, tile] = value[b * size : (b + 1) * size].astype(out.dtype)


def line_sum_kernel(own, one, two, three, total, *sent):
    value = own[...] + one[...].astype(F32) + two[...].astype(F32) + three[...].astype(F32)
    tokens = total.shape[0]
    total[...] = value[:tokens]
    for i, out in enumerate(sent, 1):
        out[...] = value[i * tokens : (i + 1) * tokens].astype(BF16)


def last_sum_kernel(own, one, two, three, out):
    value = own[...] + one[...].astype(F32) + two[...].astype(F32) + three[...].astype(F32)
    out[...] = value.astype(BF16)


def fetch_kernel(source, follow, out, done):
    del follow
    copy = pltpu.make_async_copy(source, out, done)
    copy.start()
    copy.wait()


def fetch(weight, follow):
    return pl.pallas_call(
        fetch_kernel,
        out_shape=pltpu.VMEM(weight.shape, weight.dtype),
        in_specs=[pl.BlockSpec(memory_space=pltpu.HBM), pl.BlockSpec(memory_space=pl.ANY)],
        out_specs=pl.BlockSpec(memory_space=pltpu.VMEM),
        scratch_shapes=[pltpu.SemaphoreType.DMA],
        compiler_params=pltpu.CompilerParams(vmem_limit_bytes=MIB),
        cost_estimate=pl.CostEstimate(flops=0, bytes_accessed=0, transcendentals=0),
    )(weight, follow)


def grad_in_kernel(a, b, c, d, mine, other, _, out, bias, left, right):
    @pl.when(pl.program_id(0) == 0)
    def _():
        size = a.shape[0]
        for i, slab in enumerate((a, b, c, d)):
            left[i * size : (i + 1) * size, :] = slab[...]
        join(mine, other, right)
        bias[...] = jnp.sum(right[...].astype(F32), axis=0, keepdims=True)

    out[...] = lax.dot_general(
        left[:, span(pl.program_id(0), out.shape[0])],
        right[...],
        (((0,), (0,)), ((), ())),
        preferred_element_type=F32,
    ).astype(BF16)


def grad_in(slabs, halves, follow):
    every, features = 4 * slabs[0].shape[0], slabs[0].shape[1]
    hidden = 2 * halves[0].shape[1]
    spec = pl.BlockSpec(memory_space=pltpu.VMEM)
    args = [pltpu.with_memory_space_constraint(a, pltpu.VMEM) for a in [*slabs, *halves]]
    return pl.pallas_call(
        grad_in_kernel,
        grid=(features // (2 * TILE),),
        out_shape=[
            jax.ShapeDtypeStruct((features, hidden), BF16),
            jax.ShapeDtypeStruct((1, hidden), F32),
        ],
        in_specs=[spec] * 6 + [pl.BlockSpec(memory_space=pl.ANY)],
        out_specs=[
            pl.BlockSpec((2 * TILE, hidden), lambda i: (i, 0)),
            pl.BlockSpec((1, hidden), lambda i: (0, 0)),
        ],
        scratch_shapes=[pltpu.VMEM((every, features), BF16), pltpu.VMEM((every, hidden), BF16)],
        compiler_params=pltpu.CompilerParams(vmem_limit_bytes=20 * MIB),
        cost_estimate=pl.CostEstimate(
            flops=0, bytes_accessed=0, transcendentals=0
        ),
    )(*args, follow)


def grad_out_kernel(own, *refs):
    slabs, value = refs[:4], refs[4]
    out, done, left, right, tiles, sems = refs[-6:]
    size = slabs[0].shape[0]
    core = lax.axis_index("row") & 1
    for i, slab in enumerate(slabs):
        rows = slice(i * size, (i + 1) * size)
        right[rows, :] = slab[...]
        left[rows, :] = value[rows, :] if own else swapped_rows(value, i, size // 4)
    half, width = value.shape[1], tiles.shape[2]
    place_in = span(core if own else 1 - core, half)
    copies = []
    for n in range(tiles.shape[0]):
        part = slice(n * width, (n + 1) * width)
        tiles[n] = lax.dot_general(
            left[...], right[:, part], (((0,), (0,)), ((), ())), preferred_element_type=F32
        ).astype(BF16)
        copies.append(pltpu.make_async_copy(tiles.at[n], out.at[place_in, part], sems.at[n]))
        copies[-1].start()
    done[...] = jnp.zeros_like(done)
    for copy in copies:
        copy.wait()


def grad_out(slabs, value, before=None):
    every, half = value.shape
    features = slabs[0].shape[1]
    parts = features // (2 * TILE)
    spec, whole = pl.BlockSpec(memory_space=pltpu.VMEM), pl.BlockSpec(memory_space=pltpu.HBM)
    args = [pltpu.with_memory_space_constraint(a, pltpu.VMEM) for a in [*slabs, value]]
    extra = [] if before is None else [before]
    return pl.pallas_call(
        functools.partial(grad_out_kernel, before is None),
        out_shape=[
            jax.ShapeDtypeStruct((2 * half, features), BF16),
            pltpu.VMEM((8, 128), F32),
        ],
        in_specs=[spec] * 5 + [whole] * len(extra),
        out_specs=[whole, spec],
        scratch_shapes=[
            pltpu.VMEM((every, half), BF16),
            pltpu.VMEM((every, features), BF16),
            pltpu.VMEM((parts, half, features // parts), BF16),
            pltpu.SemaphoreType.DMA((parts,)),
        ],
        input_output_aliases={5: 0} if extra else {},
        compiler_params=pltpu.CompilerParams(vmem_limit_bytes=20 * MIB),
        cost_estimate=pl.CostEstimate(
            flops=0, bytes_accessed=0, transcendentals=0
        ),
    )(*args, *extra)


def body(inputs, out_grad, w_in, bias_in, w_out):
    tokens, features = inputs.shape
    hidden = w_in.shape[1]
    half, every, line = hidden // 2, 16 * tokens, 4 * tokens
    work = 2 * every * features * half

    mine = jnp.stack([inputs, out_grad])
    steps = ring(mine, along_first)
    ins, grads = local(line_kernel, [((line, features), BF16)] * 2, steps[::-1] + [mine])
    ins = [ins] + ring(ins, along_second)
    grads = [grads] + ring(grads, along_second)

    w_in = fetch(w_in, ins[0])
    give, keep = ((every, half), BF16), ((every, half), F32)
    pre_give, pre_keep = local(
        functools.partial(product_kernel, False, (1, 0)), [give, keep], ins[::-1] + [w_in], 16, 2 * work
    )
    quarter = (every // Z, half)

    def first_sum(given, kept, follow=()):
        sent, own, near = local(
            first_sum_kernel,
            [((2,) + quarter, BF16), (quarter, F32), (quarter, F32)],
            [kept, send(given, OTHER_CORE)],
            follow=follow,
        )
        return sent, [own, near, send(sent, Z_ONE)]

    pre_sums = first_sum(pre_give, pre_keep)[1]
    (act_give,) = local(
        functools.partial(product_kernel, True, (1,)), [give], grads[::-1] + [w_out], 16, work, [pre_give]
    )
    (act_keep,) = local(
        functools.partial(product_kernel, True, (0,)), [keep], grads[::-1] + [w_out], 16, work
    )
    sums = pre_sums + first_sum(act_give, act_keep)[1]
    sent, pre, act = local(
        second_sum_kernel, [((2,) + quarter, BF16), (quarter, F32), (quarter, F32)], sums
    )
    activated, pre_grad = local(
        activate_kernel, [(quarter, BF16)] * 2, [pre, act, send(sent, Z_TWO), bias_in[None, :]]
    )

    def paired(value, near, follow=()):
        return local(pair_kernel, [((2,) + quarter, BF16)], [value, near], follow=follow)[0]

    def placed(value, near, far, follow=()):
        return local(place_kernel, [((every, half), BF16)], [value, near, far], follow=follow)[0]

    pg_near = send(pre_grad, Z_TWO)
    pg_far = send(paired(pre_grad, pg_near), Z_ONE)
    act_near = send(activated, Z_TWO)
    act_far = send(paired(activated, act_near), Z_ONE)
    pg_mine = placed(pre_grad, pg_near, pg_far, [act_near])
    pg_other = send(pg_mine, OTHER_CORE)
    (partial,) = local(share_own_kernel, [((every, features), F32)], [pg_mine, w_in], 16, work)
    share = local(
        share_other_kernel,
        [((line, features), F32)] + [((line, features), BF16)] * 3,
        [partial, pg_other, w_in],
        16,
        work,
    )
    got = [send(share[b], along_second(4 - b)) for b in (1, 2, 3)]

    grad_w_in, grad_bias = grad_in(ins, (pg_mine, pg_other), share[1])
    act_mine = placed(activated, act_near, act_far, [share[1]])
    act_other = send(act_mine, OTHER_CORE)
    grad_w_out, half_done = grad_out(grads, act_mine)

    total, *sent = local(
        line_sum_kernel,
        [((tokens, features), F32)] + [((tokens, features), BF16)] * 3,
        [share[0]] + got,
        follow=[grad_bias],
    )
    grad_w_out, done = grad_out(grads, act_other, grad_w_out)
    (grad_inputs,) = local(
        last_sum_kernel,
        [((tokens, features), BF16)],
        [total] + [send(sent[a - 1], along_first(4 - a)) for a in (1, 2, 3)],
        follow=[done],
        result=jax.ShapeDtypeStruct,
    )
    return (grad_inputs, grad_w_in, grad_bias[0].astype(BF16), grad_w_out)


def solution(mesh):
    in_specs = (
        P(("col", "dp"), "row"),
        P(("col", "dp"), "row"),
        P("row", ("col", "dp")),
        P(("col", "dp")),
        P(("col", "dp"), "row"),
    )
    out_specs = (
        P(("col", "dp"), "row"),
        P("row", ("col", "dp")),
        P(("col", "dp")),
        P(("col", "dp"), "row"),
    )
    return jax.shard_map(body, mesh=mesh, in_specs=in_specs, out_specs=out_specs, check_vma=False)
```

```python
import functools

import jax
import jax.numpy as jnp
from jax import lax
from jax.experimental import pallas as pl
from jax.experimental.pallas import tpu as pltpu
from jax.sharding import PartitionSpec as P

AXES = ("row", "col", "dp")
Z, CORES, X, Y = 4, 2, 4, 4
BF16, F32 = jnp.bfloat16, jnp.float32
SIGN = 1
TILE = 256
MIB = 1 << 20
LONG = 60 * 10**9


def place(z, core, x, y):
    return ((z * CORES + core) * 8 + x * 2 + y % 2) * 2 + y // 2


def pairs(source):
    every = [(z, c, x, y) for z in range(Z) for c in range(CORES) for x in range(X) for y in range(Y)]
    return [(place(*source(*at)), place(*at)) for at in every]


def along_first(step):
    step = SIGN * step
    return pairs(lambda z, c, x, y: (z, c, x, (y + step) % Y) if c else (z, c, (x + step) % X, y))


def along_second(step):
    step = SIGN * step
    return pairs(lambda z, c, x, y: (z, c, (x + step) % X, y) if c else (z, c, x, (y + step) % Y))


Z_ONE = pairs(lambda z, c, x, y: (z ^ (3 if c else 1), c, x, y))
Z_TWO = pairs(lambda z, c, x, y: (z ^ (1 if c else 3), c, x, y))
OTHER_CORE = pairs(lambda z, c, x, y: (z, 1 - c, x, y))


def send(value, perm):
    return lax.ppermute(value, AXES, perm)


def ring(value, along):
    return [send(value, along(d)) for d in (3, 2, 1)][::-1]


def local(kernel, outs, args, limit=8, flops=0, follow=(), result=pltpu.VMEM):
    spec = pl.BlockSpec(memory_space=pltpu.VMEM)
    count = len(args)

    def run(*refs):
        kernel(*refs[:count], *refs[count + len(follow) :])

    args = [pltpu.with_memory_space_constraint(a, pltpu.VMEM) for a in args]
    moved = sum(a.size * a.dtype.itemsize for a in args)
    return pl.pallas_call(
        run,
        out_shape=[result(shape, dtype) for shape, dtype in outs],
        in_specs=[spec] * count + [pl.BlockSpec(memory_space=pltpu.HBM if f.size > 2**20 else pl.ANY) for f in follow],
        out_specs=[spec] * len(outs),
        compiler_params=pltpu.CompilerParams(vmem_limit_bytes=limit * MIB),
        cost_estimate=pl.CostEstimate(flops=flops, bytes_accessed=0, transcendentals=0),
    )(*args, *follow)


def at():
    row = lax.axis_index("row")
    z, core = row >> 1, row & 1
    return z, core, z ^ (1 + 2 * core), z ^ (3 - 2 * core)


def span(index, size):
    return pl.ds(pl.multiple_of(index * size, size), size)


def swapped_rows(ref, block, tokens):
    return jnp.concatenate([ref[span(a * 4 + block, tokens), :] for a in range(4)], axis=0)


def line_kernel(last, far, near, mine, ins, grads):
    tokens = mine.shape[1]
    for i, ref in enumerate((mine, near, far, last)):
        ins[i * tokens : (i + 1) * tokens, :] = ref[0]
        grads[i * tokens : (i + 1) * tokens, :] = ref[1]


def mark_kernel(out):
    out[...] = jnp.zeros_like(out)


def product_kernel(transposed, halves, d, c, b, a, weight, *outs):
    core = lax.axis_index("row") & 1
    rows = jnp.concatenate([a[...], b[...], c[...], d[...]], axis=0)
    for half, out in zip(halves, outs):
        tiles = out.shape[1] // TILE
        for n in range(tiles):
            part = span((core ^ half) * tiles + n, TILE)
            if transposed:
                value = lax.dot_general(
                    rows, weight[part, :], (((1,), (1,)), ((), ())), preferred_element_type=F32
                )
            else:
                value = jnp.dot(rows, weight[:, part], preferred_element_type=F32)
            out[:, n * TILE : (n + 1) * TILE] = value.astype(out.dtype)


def first_sum_kernel(keep, got, sent, mine, near):
    z, _, one, two = at()
    size = mine.shape[0]

    def block(index):
        return keep[span(index, size), :] + swapped_rows(got, index, size // 4).astype(F32)

    sent[0] = block(one).astype(BF16)
    sent[1] = block(z ^ 2).astype(BF16)
    near[...] = block(two)
    mine[...] = block(z)


def pre_sum_kernel(mine, near, got, sent, out):
    sent[...] = (near[...] + got[1].astype(F32)).astype(BF16)
    out[...] = mine[...] + got[0].astype(F32)


def act_sum_kernel(mine, near, got, pre_sent, sent, out):
    sent[0] = pre_sent[...]
    sent[1] = (near[...] + got[1].astype(F32)).astype(BF16)
    out[...] = mine[...] + got[0].astype(F32)


def gelu_parts(value):
    scale = 0.7978845608028654
    inner = jnp.tanh(scale * (value + 0.044715 * value * value * value))
    slope = 0.5 * (1.0 + inner) + 0.5 * value * (1.0 - inner * inner) * (
        scale * (1.0 + 3.0 * 0.044715 * value * value)
    )
    return 0.5 * value * (1.0 + inner), slope


def activate_kernel(pre, act, got, bias, activated, pre_grad):
    core = lax.axis_index("row") & 1
    value = pre[...] + got[0].astype(F32) + bias[:, span(core, pre.shape[1])]
    result, slope = gelu_parts(value)
    activated[...] = result.astype(BF16)
    pre_grad[...] = ((act[...] + got[1].astype(F32)) * slope).astype(BF16)


def pair_kernel(own, near, out):
    out[0] = own[...]
    out[1] = near[...]


def place_kernel(own, near, far, out):
    z, _, one, two = at()
    size = own.shape[0]
    out[span(z, size), :] = own[...]
    out[span(two, size), :] = near[...]
    out[span(one, size), :] = far[0]
    out[span(z ^ 2, size), :] = far[1]


def orders_kernel(d, c, b, a, own, other):
    size = a.shape[0]
    tokens = size // 4
    for i, slab in enumerate((a, b, c, d)):
        own[i * size : (i + 1) * size, :] = slab[...]
        for k in range(4):
            other[k * size + i * tokens : k * size + (i + 1) * tokens, :] = slab[k * tokens : (k + 1) * tokens, :]


def share_own_kernel(mine, weight, out):
    core = lax.axis_index("row") & 1
    for n in range(out.shape[1] // TILE):
        tile = slice(n * TILE, (n + 1) * TILE)
        out[:, tile] = lax.dot_general(
            mine[...],
            weight[tile, span(core, mine.shape[1])],
            (((1,), (1,)), ((), ())),
            preferred_element_type=F32,
        )


def share_other_kernel(partial, other, weight, *outs):
    core = lax.axis_index("row") & 1
    size = outs[0].shape[0]
    rows = jnp.concatenate([swapped_rows(other, b, size // 4) for b in range(4)], axis=0)
    for n in range(partial.shape[1] // TILE):
        tile = slice(n * TILE, (n + 1) * TILE)
        value = partial[:, tile] + lax.dot_general(
            rows,
            weight[tile, span(1 - core, other.shape[1])],
            (((1,), (1,)), ((), ())),
            preferred_element_type=F32,
        )
        for b, out in enumerate(outs):
            out[:, tile] = value[b * size : (b + 1) * size].astype(out.dtype)


def line_sum_kernel(own, one, two, three, total, *sent):
    value = own[...] + one[...].astype(F32) + two[...].astype(F32) + three[...].astype(F32)
    tokens = total.shape[0]
    total[...] = value[:tokens]
    for i, out in enumerate(sent, 1):
        out[...] = value[i * tokens : (i + 1) * tokens].astype(BF16)


def last_sum_kernel(own, one, two, three, out):
    value = own[...] + one[...].astype(F32) + two[...].astype(F32) + three[...].astype(F32)
    out[...] = value.astype(BF16)


def fetch_kernel(source, follow, out, done):
    del follow
    copy = pltpu.make_async_copy(source, out, done)
    copy.start()
    copy.wait()


def fetch(weight, follow):
    return pl.pallas_call(
        fetch_kernel,
        out_shape=pltpu.VMEM(weight.shape, weight.dtype),
        in_specs=[pl.BlockSpec(memory_space=pltpu.HBM), pl.BlockSpec(memory_space=pl.ANY)],
        out_specs=pl.BlockSpec(memory_space=pltpu.VMEM),
        scratch_shapes=[pltpu.SemaphoreType.DMA],
        compiler_params=pltpu.CompilerParams(vmem_limit_bytes=MIB),
        cost_estimate=pl.CostEstimate(flops=0, bytes_accessed=0, transcendentals=0),
    )(weight, follow)


def grad_kernel(to_columns, left_own, left_other, right_own, right_other, *refs):
    out, total, tiles, sems = refs[-4:]
    core = lax.axis_index("row") & 1
    copies = []
    for i, (left, right) in enumerate(((left_own, right_own), (left_other, right_other))):
        half = core ^ i
        if to_columns:
            size = right.shape[1]
            total[:, span(half, size)] = jnp.sum(right[...].astype(F32), axis=0, keepdims=True)
        else:
            size = left.shape[1]
            total[...] = jnp.zeros_like(total)
        parts = tiles.shape[0] // 2
        width = tiles.shape[2]
        for n in range(parts):
            slot = i * parts + n
            part = slice(n * width, (n + 1) * width)
            tiles[slot] = lax.dot_general(
                left[...], right[:, part], (((0,), (0,)), ((), ())), preferred_element_type=F32
            ).astype(BF16)
            if to_columns:
                target = out.at[:, span(half * parts + n, width)]
            else:
                target = out.at[span(half, size), part]
            copies.append(pltpu.make_async_copy(tiles.at[slot], target, sems.at[slot]))
            copies[-1].start()
    for copy in copies:
        copy.wait()


def grad_of(left, right, to_columns, follow):
    every, rows = left[0].shape
    columns = right[0].shape[1]
    shape = (rows, 2 * columns) if to_columns else (2 * rows, columns)
    width = columns // (2 if to_columns else 3)
    parts = 2 * columns // width
    spec, whole = pl.BlockSpec(memory_space=pltpu.VMEM), pl.BlockSpec(memory_space=pltpu.HBM)
    args = [pltpu.with_memory_space_constraint(a, pltpu.VMEM) for a in [*left, *right]]
    return pl.pallas_call(
        functools.partial(grad_kernel, to_columns),
        out_shape=[jax.ShapeDtypeStruct(shape, BF16), pltpu.VMEM((1, shape[1]), F32)],
        in_specs=[spec] * 4 + [pl.BlockSpec(memory_space=pl.ANY)] * len(follow),
        out_specs=[whole, spec],
        scratch_shapes=[pltpu.VMEM((parts, rows, width), BF16), pltpu.SemaphoreType.DMA((parts,))],
        compiler_params=pltpu.CompilerParams(vmem_limit_bytes=20 * MIB),
        cost_estimate=pl.CostEstimate(flops=0, bytes_accessed=0, transcendentals=0),
    )(*args, *follow)


def both_orders(slabs):
    whole = ((4 * slabs[0].shape[0], slabs[0].shape[1]), BF16)
    return local(orders_kernel, [whole] * 2, slabs[::-1])


def body(inputs, out_grad, w_in, bias_in, w_out):
    tokens, features = inputs.shape
    hidden = w_in.shape[1]
    half, every, line = hidden // 2, 16 * tokens, 4 * tokens

    mine = jnp.stack([inputs, out_grad])
    steps = ring(mine, along_first)
    ins, grads = local(line_kernel, [((line, features), BF16)] * 2, steps[::-1] + [mine])
    ins = [ins] + ring(ins, along_second)
    grads = [grads] + ring(grads, along_second)

    w_in = fetch(w_in, ins[0])
    give, keep = ((every, half), BF16), ((every, half), F32)
    pre_give, pre_keep = local(
        functools.partial(product_kernel, False, (1, 0)), [give, keep], ins[::-1] + [w_in], 16, 0
    )
    quarter = (every // Z, half)

    def first_sum(given, kept, follow=()):
        sent, own, near = local(
            first_sum_kernel,
            [((2,) + quarter, BF16), (quarter, F32), (quarter, F32)],
            [kept, send(given, OTHER_CORE)],
            follow=follow,
        )
        return sent, [own, near, send(sent, Z_ONE)]

    (arrived,) = local(mark_kernel, [((8, 128), F32)], [], flops=LONG, follow=grads[1:])
    pre_sent, pre_sums = first_sum(pre_give, pre_keep, [arrived])
    (act_give,) = local(
        functools.partial(product_kernel, True, (1,)), [give], grads[::-1] + [w_out], 16, 0, [pre_sent]
    )
    (act_keep,) = local(
        functools.partial(product_kernel, True, (0,)), [keep], grads[::-1] + [w_out], 16, 0
    )
    act_sums = first_sum(act_give, act_keep)[1]
    in_orders = both_orders(ins)
    grad_orders = both_orders(grads)
    pre_last, pre = local(
        pre_sum_kernel, [(quarter, BF16), (quarter, F32)], pre_sums, flops=LONG
    )
    sent, act = local(
        act_sum_kernel,
        [((2,) + quarter, BF16), (quarter, F32)],
        act_sums + [pre_last],
        follow=in_orders[:1] + grad_orders[:1],
    )
    activated, pre_grad = local(
        activate_kernel, [(quarter, BF16)] * 2, [pre, act, send(sent, Z_TWO), bias_in[None, :]]
    )

    def paired(value, near, follow=()):
        return local(pair_kernel, [((2,) + quarter, BF16)], [value, near], follow=follow)[0]

    def placed(value, near, far, follow=()):
        return local(place_kernel, [((every, half), BF16)], [value, near, far], follow=follow)[0]

    pg_near = send(pre_grad, Z_TWO)
    pg_far = send(paired(pre_grad, pg_near), Z_ONE)
    act_near = send(activated, Z_TWO)
    act_far = send(paired(activated, act_near), Z_ONE)
    pg_mine = placed(pre_grad, pg_near, pg_far, [act_near])
    pg_other = send(pg_mine, OTHER_CORE)
    (partial,) = local(share_own_kernel, [((every, features), F32)], [pg_mine, w_in], 16, 0)
    share = local(
        share_other_kernel,
        [((line, features), F32)] + [((line, features), BF16)] * 3,
        [partial, pg_other, w_in],
        16,
        0,
    )
    got = [send(share[b], along_second(4 - b)) for b in (1, 2, 3)]

    grad_w_in, grad_bias = grad_of(in_orders, (pg_mine, pg_other), True, [share[1]])
    grad_bias = grad_bias[0].astype(BF16)
    total, *sent = local(
        line_sum_kernel,
        [((tokens, features), F32)] + [((tokens, features), BF16)] * 3,
        [share[0]] + got,
        follow=[grad_bias],
    )
    act_mine = placed(activated, act_near, act_far, [total])
    act_other = send(act_mine, OTHER_CORE)
    grad_w_out, done = grad_of((act_mine, act_other), grad_orders, False, [])
    (grad_inputs,) = local(
        last_sum_kernel,
        [((tokens, features), BF16)],
        [total] + [send(sent[a - 1], along_first(4 - a)) for a in (1, 2, 3)],
        follow=[done],
        result=jax.ShapeDtypeStruct,
    )
    return (grad_inputs, grad_w_in, grad_bias, grad_w_out)


def solution(mesh):
    in_specs = (
        P(("col", "dp"), "row"),
        P(("col", "dp"), "row"),
        P("row", ("col", "dp")),
        P(("col", "dp")),
        P(("col", "dp"), "row"),
    )
    out_specs = (
        P(("col", "dp"), "row"),
        P("row", ("col", "dp")),
        P(("col", "dp")),
        P(("col", "dp"), "row"),
    )
    return jax.shard_map(body, mesh=mesh, in_specs=in_specs, out_specs=out_specs, check_vma=False)
```

```python
import functools

import jax
import jax.numpy as jnp
from jax import lax
from jax.experimental import pallas as pl
from jax.experimental.pallas import tpu as pltpu
from jax.sharding import PartitionSpec as P

AXES = ("row", "col", "dp")
Z, CORES, X, Y = 4, 2, 4, 4
BF16, F32 = jnp.bfloat16, jnp.float32
STEPS = (0, 1, 3, 2)
TILE = 256
MIB = 1 << 20
LONG = 60 * 10**9


def place(z, core, x, y):
    return ((z * CORES + core) * 8 + x * 2 + y % 2) * 2 + y // 2


def pairs(source):
    every = [(z, c, x, y) for z in range(Z) for c in range(CORES) for x in range(X) for y in range(Y)]
    return [(place(*source(*at)), place(*at)) for at in every]


def along_first(step):
    return pairs(lambda z, c, x, y: (z, c, x, (y + step) % Y) if c else (z, c, (x + step) % X, y))


def along_second(step):
    return pairs(lambda z, c, x, y: (z, c, (x + step) % X, y) if c else (z, c, x, (y + step) % Y))


Z_ONE = pairs(lambda z, c, x, y: (z ^ (3 if c else 1), c, x, y))
Z_TWO = pairs(lambda z, c, x, y: (z ^ (1 if c else 3), c, x, y))


def along_z(step):
    return pairs(lambda z, c, x, y: ((z + step) % Z, c, x, y))


OTHER_CORE = pairs(lambda z, c, x, y: (z, 1 - c, x, y))


def send(value, perm):
    return lax.ppermute(value, AXES, perm)


def ring(value, along):
    return [send(value, along(STEPS[i])) for i in (3, 2, 1)][::-1]


def local(kernel, outs, args, limit=8, flops=0, follow=(), result=pltpu.VMEM):
    spec = pl.BlockSpec(memory_space=pltpu.VMEM)
    count = len(args)

    def run(*refs):
        kernel(*refs[:count], *refs[count + len(follow) :])

    args = [pltpu.with_memory_space_constraint(a, pltpu.VMEM) for a in args]
    moved = sum(a.size * a.dtype.itemsize for a in args)
    return pl.pallas_call(
        run,
        out_shape=[result(shape, dtype) for shape, dtype in outs],
        in_specs=[spec] * count + [pl.BlockSpec(memory_space=pltpu.HBM if f.size > 2**20 else pl.ANY) for f in follow],
        out_specs=[spec] * len(outs),
        compiler_params=pltpu.CompilerParams(vmem_limit_bytes=limit * MIB),
        cost_estimate=pl.CostEstimate(flops=flops, bytes_accessed=0, transcendentals=0),
    )(*args, *follow)


def at():
    row = lax.axis_index("row")
    z, core = row >> 1, row & 1
    return z, core, z ^ (1 + 2 * core), z ^ (3 - 2 * core)


def span(index, size):
    return pl.ds(pl.multiple_of(index * size, size), size)


def swapped_rows(ref, block, tokens):
    return jnp.concatenate([ref[span(a * 4 + block, tokens), :] for a in range(4)], axis=0)


def line_kernel(last, far, near, mine, ins, grads):
    tokens = mine.shape[1]
    for i, ref in enumerate((mine, near, far, last)):
        ins[i * tokens : (i + 1) * tokens, :] = ref[0]
        grads[i * tokens : (i + 1) * tokens, :] = ref[1]


def mark_kernel(out):
    out[...] = jnp.zeros_like(out)


def product_kernel(transposed, halves, d, c, b, a, weight, *outs):
    core = lax.axis_index("row") & 1
    rows = jnp.concatenate([a[...], b[...], c[...], d[...]], axis=0)
    for half, out in zip(halves, outs):
        tiles = out.shape[1] // TILE
        for n in range(tiles):
            part = span((core ^ half) * tiles + n, TILE)
            if transposed:
                value = lax.dot_general(
                    rows, weight[part, :], (((1,), (1,)), ((), ())), preferred_element_type=F32
                )
            else:
                value = jnp.dot(rows, weight[:, part], preferred_element_type=F32)
            out[:, n * TILE : (n + 1) * TILE] = value.astype(out.dtype)


def first_sum_kernel(keep, got, sent, mine, near):
    z, _, one, two = at()
    size = mine.shape[0]

    def block(index):
        return keep[span(index, size), :] + swapped_rows(got, index, size // 4).astype(F32)

    sent[0] = block(one).astype(BF16)
    sent[1] = block(z ^ 2).astype(BF16)
    near[...] = block(two)
    mine[...] = block(z)


def second_sum_kernel(mine, near, got, sent, out):
    sent[...] = (near[...] + got[1].astype(F32)).astype(BF16)
    out[...] = mine[...] + got[0].astype(F32)


def gelu_parts(value):
    scale = 0.7978845608028654
    inner = jnp.tanh(scale * (value + 0.044715 * value * value * value))
    slope = 0.5 * (1.0 + inner) + 0.5 * value * (1.0 - inner * inner) * (
        scale * (1.0 + 3.0 * 0.044715 * value * value)
    )
    return 0.5 * value * (1.0 + inner), slope


def activate_kernel(mine, got, bias, activated, slope):
    core = lax.axis_index("row") & 1
    value = mine[...] + got[...].astype(F32) + bias[:, span(core, mine.shape[1])]
    result, derivative = gelu_parts(value)
    activated[...] = result.astype(BF16)
    slope[...] = derivative


def pre_grad_kernel(mine, got, slope, out):
    out[...] = ((mine[...] + got[...].astype(F32)) * slope[...]).astype(BF16)


def pair_kernel(own, near, out):
    out[0] = own[...]
    out[1] = near[...]


def place_ring_kernel(two, three, one, own, out):
    z, size = at()[0], own.shape[0]
    for step, ref in enumerate((own, one, two, three)):
        out[span((z + step) & 3, size), :] = ref[...]


def copy_kernel(value, out):
    out[...] = value[...]


def place_kernel(own, near, far, out):
    z, _, one, two = at()
    size = own.shape[0]
    out[span(z, size), :] = own[...]
    out[span(two, size), :] = near[...]
    out[span(one, size), :] = far[0]
    out[span(z ^ 2, size), :] = far[1]


def orders_kernel(d, c, b, a, own, other):
    size = a.shape[0]
    tokens = size // 4
    for i, slab in enumerate((a, b, c, d)):
        own[i * size : (i + 1) * size, :] = slab[...]
        for k in range(4):
            other[k * size + i * tokens : k * size + (i + 1) * tokens, :] = slab[k * tokens : (k + 1) * tokens, :]


def share_own_kernel(mine, weight, out):
    core = lax.axis_index("row") & 1
    for n in range(out.shape[1] // TILE):
        tile = slice(n * TILE, (n + 1) * TILE)
        out[:, tile] = lax.dot_general(
            mine[...],
            weight[tile, span(core, mine.shape[1])],
            (((1,), (1,)), ((), ())),
            preferred_element_type=F32,
        )


def share_other_kernel(partial, other, weight, *outs):
    core = lax.axis_index("row") & 1
    size = outs[0].shape[0]
    rows = jnp.concatenate([swapped_rows(other, b, size // 4) for b in range(4)], axis=0)
    for n in range(partial.shape[1] // TILE):
        tile = slice(n * TILE, (n + 1) * TILE)
        value = partial[:, tile] + lax.dot_general(
            rows,
            weight[tile, span(1 - core, other.shape[1])],
            (((1,), (1,)), ((), ())),
            preferred_element_type=F32,
        )
        for b, out in enumerate(outs):
            out[:, tile] = value[b * size : (b + 1) * size].astype(out.dtype)


def line_sum_kernel(three, two, one, own, total, *sent):
    value = own[...] + one[...].astype(F32) + two[...].astype(F32) + three[...].astype(F32)
    tokens = total.shape[0]
    total[...] = value[:tokens]
    for i, out in enumerate(sent, 1):
        out[...] = value[i * tokens : (i + 1) * tokens].astype(BF16)


def last_sum_kernel(three, two, one, own, out):
    value = own[...] + one[...].astype(F32) + two[...].astype(F32) + three[...].astype(F32)
    out[...] = value.astype(BF16)


def fetch_kernel(source, follow, out, done):
    del follow
    copy = pltpu.make_async_copy(source, out, done)
    copy.start()
    copy.wait()


def fetch(weight, follow):
    return pl.pallas_call(
        fetch_kernel,
        out_shape=pltpu.VMEM(weight.shape, weight.dtype),
        in_specs=[pl.BlockSpec(memory_space=pltpu.HBM), pl.BlockSpec(memory_space=pl.ANY)],
        out_specs=pl.BlockSpec(memory_space=pltpu.VMEM),
        scratch_shapes=[pltpu.SemaphoreType.DMA],
        compiler_params=pltpu.CompilerParams(vmem_limit_bytes=MIB),
        cost_estimate=pl.CostEstimate(flops=0, bytes_accessed=0, transcendentals=0),
    )(weight, follow)


def grad_kernel(to_columns, left_own, left_other, right_own, right_other, *refs):
    out, total, tiles, sems = refs[-4:]
    core = lax.axis_index("row") & 1
    copies = []
    for i, (left, right) in enumerate(((left_own, right_own), (left_other, right_other))):
        half = core ^ i
        if to_columns:
            size = right.shape[1]
            total[:, span(half, size)] = jnp.sum(right[...].astype(F32), axis=0, keepdims=True)
        else:
            size = left.shape[1]
            total[...] = jnp.zeros_like(total)
        parts = tiles.shape[0] // 2
        width = tiles.shape[2]
        for n in range(parts):
            slot = i * parts + n
            part = slice(n * width, (n + 1) * width)
            tiles[slot] = lax.dot_general(
                left[...], right[:, part], (((0,), (0,)), ((), ())), preferred_element_type=F32
            ).astype(BF16)
            if to_columns:
                target = out.at[:, span(half * parts + n, width)]
            else:
                target = out.at[span(half, size), part]
            copies.append(pltpu.make_async_copy(tiles.at[slot], target, sems.at[slot]))
            copies[-1].start()
    for copy in copies:
        copy.wait()


def grad_of(left, right, to_columns, follow):
    every, rows = left[0].shape
    columns = right[0].shape[1]
    shape = (rows, 2 * columns) if to_columns else (2 * rows, columns)
    width = columns // (2 if to_columns else 3)
    parts = 2 * columns // width
    spec, whole = pl.BlockSpec(memory_space=pltpu.VMEM), pl.BlockSpec(memory_space=pltpu.HBM)
    args = [pltpu.with_memory_space_constraint(a, pltpu.VMEM) for a in [*left, *right]]
    return pl.pallas_call(
        functools.partial(grad_kernel, to_columns),
        out_shape=[jax.ShapeDtypeStruct(shape, BF16), pltpu.VMEM((1, shape[1]), F32)],
        in_specs=[spec] * 4 + [pl.BlockSpec(memory_space=pl.ANY)] * len(follow),
        out_specs=[whole, spec],
        scratch_shapes=[pltpu.VMEM((parts, rows, width), BF16), pltpu.SemaphoreType.DMA((parts,))],
        compiler_params=pltpu.CompilerParams(vmem_limit_bytes=20 * MIB),
        cost_estimate=pl.CostEstimate(flops=0, bytes_accessed=0, transcendentals=0),
    )(*args, *follow)


def both_orders(slabs):
    whole = ((4 * slabs[0].shape[0], slabs[0].shape[1]), BF16)
    return local(orders_kernel, [whole] * 2, slabs[::-1])


def body(inputs, out_grad, w_in, bias_in, w_out):
    tokens, features = inputs.shape
    hidden = w_in.shape[1]
    half, every, line = hidden // 2, 16 * tokens, 4 * tokens

    mine = jnp.stack([inputs, out_grad])
    steps = ring(mine, along_first)
    ins, grads = local(line_kernel, [((line, features), BF16)] * 2, steps[::-1] + [mine])
    ins = [ins] + ring(ins, along_second)
    grads = [grads] + ring(grads, along_second)

    w_in = fetch(w_in, ins[0])
    give, keep = ((every, half), BF16), ((every, half), F32)
    pre_give, pre_keep = local(
        functools.partial(product_kernel, False, (1, 0)), [give, keep], ins[::-1] + [w_in], 16, 0
    )
    quarter = (every // Z, half)

    def first_sum(given, kept, follow=()):
        sent, own, near = local(
            first_sum_kernel,
            [((2,) + quarter, BF16), (quarter, F32), (quarter, F32)],
            [kept, send(given, OTHER_CORE)],
            follow=follow,
        )
        return sent, [own, near, send(sent, Z_ONE)]

    (arrived,) = local(mark_kernel, [((8, 128), F32)], [], flops=LONG, follow=grads[1:])
    pre_sent, pre_sums = first_sum(pre_give, pre_keep, [arrived])
    (act_give,) = local(
        functools.partial(product_kernel, True, (1,)), [give], grads[::-1] + [w_out], 16, 0, [pre_sent]
    )
    (act_keep,) = local(
        functools.partial(product_kernel, True, (0,)), [keep], grads[::-1] + [w_out], 16, 0
    )
    act_sums = first_sum(act_give, act_keep)[1]
    in_orders = both_orders(ins)
    grad_orders = both_orders(grads)
    last = [(quarter, BF16), (quarter, F32)]
    pre_last, pre = local(second_sum_kernel, last, pre_sums, flops=LONG)
    activated, slope = local(
        activate_kernel, last, [pre, send(pre_last, Z_TWO), bias_in[None, :]], flops=LONG
    )
    act_last, act = local(
        second_sum_kernel, last, act_sums, follow=in_orders[:1] + grad_orders[:1]
    )
    (pre_grad,) = local(pre_grad_kernel, last[:1], [act, send(act_last, Z_TWO), slope])

    def paired(value, near, follow=()):
        return local(pair_kernel, [((2,) + quarter, BF16)], [value, near], follow=follow)[0]

    def placed(value, near, far, follow=()):
        return local(place_kernel, [((every, half), BF16)], [value, near, far], follow=follow)[0]

    def gathered(value, follow):
        return local(
            place_ring_kernel, [((every, half), BF16)], [send(value, along_z(d)) for d in (2, 3, 1)] + [value], follow=follow
        )[0]

    act_near = send(activated, Z_TWO)
    act_far = send(paired(activated, act_near), Z_ONE)
    pg_mine = gathered(pre_grad, [act_near])
    pg_other = send(pg_mine, OTHER_CORE)
    (partial,) = local(share_own_kernel, [((every, features), F32)], [pg_mine, w_in], 16, 0)
    share = local(
        share_other_kernel,
        [((line, features), F32)] + [((line, features), BF16)] * 3,
        [partial, pg_other, w_in],
        16,
        0,
    )
    got = [send(share[b], along_second(-STEPS[b])) for b in (3, 2, 1)]

    grad_w_in, grad_bias = grad_of(in_orders, (pg_mine, pg_other), True, [share[1]])
    grad_bias = grad_bias[0].astype(BF16)
    total, *sent = local(
        line_sum_kernel,
        [((tokens, features), F32)] + [((tokens, features), BF16)] * 3,
        got + [share[0]],
        follow=[grad_bias],
    )
    act_mine = placed(activated, act_near, act_far, [total])
    act_other = send(act_mine, OTHER_CORE)
    grad_w_out, done = grad_of((act_mine, act_other), grad_orders, False, [])
    (grad_inputs,) = local(
        last_sum_kernel,
        [((tokens, features), BF16)],
        [send(sent[a - 1], along_first(-STEPS[a])) for a in (3, 2, 1)] + [total],
        follow=[done],
        result=jax.ShapeDtypeStruct,
    )
    return (grad_inputs, grad_w_in, grad_bias, grad_w_out)


def solution(mesh):
    in_specs = (
        P(("col", "dp"), "row"),
        P(("col", "dp"), "row"),
        P("row", ("col", "dp")),
        P(("col", "dp")),
        P(("col", "dp"), "row"),
    )
    out_specs = (
        P(("col", "dp"), "row"),
        P("row", ("col", "dp")),
        P(("col", "dp")),
        P(("col", "dp"), "row"),
    )
    return jax.shard_map(body, mesh=mesh, in_specs=in_specs, out_specs=out_specs, check_vma=False)
```

```python
import functools

import jax
import jax.numpy as jnp
from jax import lax
from jax.experimental import pallas as pl
from jax.experimental.pallas import tpu as pltpu
from jax.sharding import PartitionSpec as P

AXES = ("row", "col", "dp")
Z, CORES, X, Y = 4, 2, 4, 4
BF16, F32 = jnp.bfloat16, jnp.float32
STEPS = (0, 1, 3, 2)
TILE = 256
MIB = 1 << 20
LONG = 60 * 10**9


def place(z, core, x, y):
    return ((z * CORES + core) * 8 + x * 2 + y % 2) * 2 + y // 2


def pairs(source):
    every = [(z, c, x, y) for z in range(Z) for c in range(CORES) for x in range(X) for y in range(Y)]
    return [(place(*source(*at)), place(*at)) for at in every]


def along_first(step):
    return pairs(lambda z, c, x, y: (z, c, x, (y + step) % Y) if c else (z, c, (x + step) % X, y))


def along_second(step):
    return pairs(lambda z, c, x, y: (z, c, (x + step) % X, y) if c else (z, c, x, (y + step) % Y))


Z_ONE = pairs(lambda z, c, x, y: (z ^ (3 if c else 1), c, x, y))
Z_TWO = pairs(lambda z, c, x, y: (z ^ (1 if c else 3), c, x, y))


def along_z(step):
    return pairs(lambda z, c, x, y: ((z + step) % Z, c, x, y))


OTHER_CORE = pairs(lambda z, c, x, y: (z, 1 - c, x, y))


def send(value, perm):
    return lax.ppermute(value, AXES, perm)


def ring(value, along):
    return [send(value, along(STEPS[i])) for i in (3, 2, 1)][::-1]


def local(kernel, outs, args, limit=8, flops=0, follow=(), result=pltpu.VMEM):
    spec = pl.BlockSpec(memory_space=pltpu.VMEM)
    count = len(args)

    def run(*refs):
        kernel(*refs[:count], *refs[count + len(follow) :])

    args = [pltpu.with_memory_space_constraint(a, pltpu.VMEM) for a in args]
    moved = sum(a.size * a.dtype.itemsize for a in args)
    return pl.pallas_call(
        run,
        out_shape=[result(shape, dtype) for shape, dtype in outs],
        in_specs=[spec] * count + [pl.BlockSpec(memory_space=pltpu.HBM if f.size > 2**20 else pl.ANY) for f in follow],
        out_specs=[spec] * len(outs),
        compiler_params=pltpu.CompilerParams(vmem_limit_bytes=limit * MIB),
        cost_estimate=pl.CostEstimate(flops=flops, bytes_accessed=0, transcendentals=0),
    )(*args, *follow)


def at():
    row = lax.axis_index("row")
    z, core = row >> 1, row & 1
    return z, core, z ^ (1 + 2 * core), z ^ (3 - 2 * core)


def span(index, size):
    return pl.ds(pl.multiple_of(index * size, size), size)


def swapped_rows(ref, block, tokens):
    return jnp.concatenate([ref[span(a * 4 + block, tokens), :] for a in range(4)], axis=0)


def line_kernel(last, far, near, mine, ins, grads):
    tokens = mine.shape[1]
    for i, ref in enumerate((mine, near, far, last)):
        ins[i * tokens : (i + 1) * tokens, :] = ref[0]
        grads[i * tokens : (i + 1) * tokens, :] = ref[1]


def mark_kernel(out):
    out[...] = jnp.zeros_like(out)


def product_kernel(transposed, halves, d, c, b, a, weight, *outs):
    core = lax.axis_index("row") & 1
    rows = jnp.concatenate([a[...], b[...], c[...], d[...]], axis=0)
    for half, out in zip(halves, outs):
        tiles = out.shape[1] // TILE
        for n in range(tiles):
            part = span((core ^ half) * tiles + n, TILE)
            if transposed:
                value = lax.dot_general(
                    rows, weight[part, :], (((1,), (1,)), ((), ())), preferred_element_type=F32
                )
            else:
                value = jnp.dot(rows, weight[:, part], preferred_element_type=F32)
            out[:, n * TILE : (n + 1) * TILE] = value.astype(out.dtype)


def first_sum_kernel(keep, got, sent, mine, near):
    z, _, one, two = at()
    size = mine.shape[0]

    def block(index):
        return keep[span(index, size), :] + swapped_rows(got, index, size // 4).astype(F32)

    sent[0] = block(one).astype(BF16)
    sent[1] = block(z ^ 2).astype(BF16)
    near[...] = block(two)
    mine[...] = block(z)


def second_sum_kernel(mine, near, got, sent, out):
    sent[...] = (near[...] + got[1].astype(F32)).astype(BF16)
    out[...] = mine[...] + got[0].astype(F32)


def gelu_parts(value):
    scale = 0.7978845608028654
    inner = jnp.tanh(scale * (value + 0.044715 * value * value * value))
    slope = 0.5 * (1.0 + inner) + 0.5 * value * (1.0 - inner * inner) * (
        scale * (1.0 + 3.0 * 0.044715 * value * value)
    )
    return 0.5 * value * (1.0 + inner), slope


def activate_kernel(mine, got, bias, activated, slope):
    core = lax.axis_index("row") & 1
    value = mine[...] + got[...].astype(F32) + bias[:, span(core, mine.shape[1])]
    result, derivative = gelu_parts(value)
    activated[...] = result.astype(BF16)
    slope[...] = derivative


def pre_grad_kernel(mine, got, slope, out):
    out[...] = ((mine[...] + got[...].astype(F32)) * slope[...]).astype(BF16)


def pair_kernel(own, near, out):
    out[0] = own[...]
    out[1] = near[...]


def place_ring_kernel(two, three, one, own, out):
    z, size = at()[0], own.shape[0]
    for step, ref in enumerate((own, one, two, three)):
        out[span((z + step) & 3, size), :] = ref[...]


def copy_kernel(value, out):
    out[...] = value[...]


def place_kernel(own, near, far, out):
    z, _, one, two = at()
    size = own.shape[0]
    out[span(z, size), :] = own[...]
    out[span(one, size), :] = near[...]
    out[span(two, size), :] = far[0]
    out[span(z ^ 2, size), :] = far[1]


def orders_kernel(d, c, b, a, own, other):
    size = a.shape[0]
    tokens = size // 4
    for i, slab in enumerate((a, b, c, d)):
        own[i * size : (i + 1) * size, :] = slab[...]
        for k in range(4):
            other[k * size + i * tokens : k * size + (i + 1) * tokens, :] = slab[k * tokens : (k + 1) * tokens, :]


def share_own_kernel(mine, weight, out):
    core = lax.axis_index("row") & 1
    for n in range(out.shape[1] // TILE):
        tile = slice(n * TILE, (n + 1) * TILE)
        out[:, tile] = lax.dot_general(
            mine[...],
            weight[tile, span(core, mine.shape[1])],
            (((1,), (1,)), ((), ())),
            preferred_element_type=F32,
        )


def share_other_kernel(partial, other, weight, *outs):
    core = lax.axis_index("row") & 1
    size = outs[0].shape[0]
    rows = jnp.concatenate([swapped_rows(other, b, size // 4) for b in range(4)], axis=0)
    for n in range(partial.shape[1] // TILE):
        tile = slice(n * TILE, (n + 1) * TILE)
        value = partial[:, tile] + lax.dot_general(
            rows,
            weight[tile, span(1 - core, other.shape[1])],
            (((1,), (1,)), ((), ())),
            preferred_element_type=F32,
        )
        for b, out in enumerate(outs):
            out[:, tile] = value[b * size : (b + 1) * size].astype(out.dtype)


def line_sum_kernel(three, two, one, own, total, *sent):
    value = own[...] + one[...].astype(F32) + two[...].astype(F32) + three[...].astype(F32)
    tokens = total.shape[0]
    total[...] = value[:tokens]
    for i, out in enumerate(sent, 1):
        out[...] = value[i * tokens : (i + 1) * tokens].astype(BF16)


def last_sum_kernel(three, two, one, own, out):
    value = own[...] + one[...].astype(F32) + two[...].astype(F32) + three[...].astype(F32)
    out[...] = value.astype(BF16)


def fetch_kernel(source, follow, out, done):
    del follow
    copy = pltpu.make_async_copy(source, out, done)
    copy.start()
    copy.wait()


def fetch(weight, follow):
    return pl.pallas_call(
        fetch_kernel,
        out_shape=pltpu.VMEM(weight.shape, weight.dtype),
        in_specs=[pl.BlockSpec(memory_space=pltpu.HBM), pl.BlockSpec(memory_space=pl.ANY)],
        out_specs=pl.BlockSpec(memory_space=pltpu.VMEM),
        scratch_shapes=[pltpu.SemaphoreType.DMA],
        compiler_params=pltpu.CompilerParams(vmem_limit_bytes=MIB),
        cost_estimate=pl.CostEstimate(flops=0, bytes_accessed=0, transcendentals=0),
    )(weight, follow)


def grad_kernel(to_columns, left_own, left_other, right_own, right_other, *refs):
    out, total, tiles, sems = refs[-4:]
    core = lax.axis_index("row") & 1
    copies = []
    for i, (left, right) in enumerate(((left_own, right_own), (left_other, right_other))):
        half = core ^ i
        if to_columns:
            size = right.shape[1]
            total[:, span(half, size)] = jnp.sum(right[...].astype(F32), axis=0, keepdims=True)
        else:
            size = left.shape[1]
            total[...] = jnp.zeros_like(total)
        parts = tiles.shape[0] // 2
        width = tiles.shape[2]
        for n in range(parts):
            slot = i * parts + n
            part = slice(n * width, (n + 1) * width)
            tiles[slot] = lax.dot_general(
                left[...], right[:, part], (((0,), (0,)), ((), ())), preferred_element_type=F32
            ).astype(BF16)
            if to_columns:
                target = out.at[:, span(half * parts + n, width)]
            else:
                target = out.at[span(half, size), part]
            copies.append(pltpu.make_async_copy(tiles.at[slot], target, sems.at[slot]))
            copies[-1].start()
    for copy in copies:
        copy.wait()


def grad_of(left, right, to_columns, follow):
    every, rows = left[0].shape
    columns = right[0].shape[1]
    shape = (rows, 2 * columns) if to_columns else (2 * rows, columns)
    width = columns // (2 if to_columns else 3)
    parts = 2 * columns // width
    spec, whole = pl.BlockSpec(memory_space=pltpu.VMEM), pl.BlockSpec(memory_space=pltpu.HBM)
    args = [pltpu.with_memory_space_constraint(a, pltpu.VMEM) for a in [*left, *right]]
    return pl.pallas_call(
        functools.partial(grad_kernel, to_columns),
        out_shape=[jax.ShapeDtypeStruct(shape, BF16), pltpu.VMEM((1, shape[1]), F32)],
        in_specs=[spec] * 4 + [pl.BlockSpec(memory_space=pl.ANY)] * len(follow),
        out_specs=[whole, spec],
        scratch_shapes=[pltpu.VMEM((parts, rows, width), BF16), pltpu.SemaphoreType.DMA((parts,))],
        compiler_params=pltpu.CompilerParams(vmem_limit_bytes=20 * MIB),
        cost_estimate=pl.CostEstimate(flops=0, bytes_accessed=0, transcendentals=0),
    )(*args, *follow)


def both_orders(slabs):
    whole = ((4 * slabs[0].shape[0], slabs[0].shape[1]), BF16)
    return local(orders_kernel, [whole] * 2, slabs[::-1])


def body(inputs, out_grad, w_in, bias_in, w_out):
    tokens, features = inputs.shape
    hidden = w_in.shape[1]
    half, every, line = hidden // 2, 16 * tokens, 4 * tokens

    mine = jnp.stack([inputs, out_grad])
    steps = ring(mine, along_first)
    ins, grads = local(line_kernel, [((line, features), BF16)] * 2, steps[::-1] + [mine])
    ins = [ins] + ring(ins, along_second)
    grads = [grads] + ring(grads, along_second)

    w_in = fetch(w_in, ins[0])
    give, keep = ((every, half), BF16), ((every, half), F32)
    pre_give, pre_keep = local(
        functools.partial(product_kernel, False, (1, 0)), [give, keep], ins[::-1] + [w_in], 16, 0
    )
    quarter = (every // Z, half)

    def first_sum(given, kept, follow=()):
        sent, own, near = local(
            first_sum_kernel,
            [((2,) + quarter, BF16), (quarter, F32), (quarter, F32)],
            [kept, send(given, OTHER_CORE)],
            follow=follow,
        )
        return sent, [own, near, send(sent, Z_ONE)]

    (arrived,) = local(mark_kernel, [((8, 128), F32)], [], flops=LONG, follow=grads[1:])
    pre_sent, pre_sums = first_sum(pre_give, pre_keep, [arrived])
    (act_give,) = local(
        functools.partial(product_kernel, True, (1,)), [give], grads[::-1] + [w_out], 16, 0, [pre_sent]
    )
    (act_keep,) = local(
        functools.partial(product_kernel, True, (0,)), [keep], grads[::-1] + [w_out], 16, 0
    )
    act_sums = first_sum(act_give, act_keep)[1]
    in_orders = both_orders(ins)
    grad_orders = both_orders(grads)
    last = [(quarter, BF16), (quarter, F32)]
    pre_last, pre = local(second_sum_kernel, last, pre_sums, flops=LONG)
    activated, slope = local(
        activate_kernel, last, [pre, send(pre_last, Z_TWO), bias_in[None, :]], flops=LONG
    )
    act_last, act = local(
        second_sum_kernel, last, act_sums, follow=in_orders[:1] + grad_orders[:1]
    )
    (pre_grad,) = local(pre_grad_kernel, last[:1], [act, send(act_last, Z_TWO), slope])

    def paired(value, near, follow=()):
        return local(pair_kernel, [((2,) + quarter, BF16)], [value, near], follow=follow)[0]

    def placed(value, near, far, follow=()):
        return local(place_kernel, [((every, half), BF16)], [value, near, far], follow=follow)[0]

    def gathered(value, follow):
        return local(
            place_ring_kernel, [((every, half), BF16)], [send(value, along_z(d)) for d in (2, 3, 1)] + [value], follow=follow
        )[0]

    act_near = send(activated, Z_ONE)
    act_far = send(paired(activated, act_near), Z_TWO)
    pg_mine = gathered(pre_grad, [act_near])
    pg_other = send(pg_mine, OTHER_CORE)
    (partial,) = local(share_own_kernel, [((every, features), F32)], [pg_mine, w_in], 16, 0)
    share = local(
        share_other_kernel,
        [((line, features), F32)] + [((line, features), BF16)] * 3,
        [partial, pg_other, w_in],
        16,
        0,
    )
    got = [send(share[b], along_second(-STEPS[b])) for b in (3, 2, 1)]

    grad_w_in, grad_bias = grad_of(in_orders, (pg_mine, pg_other), True, [share[1]])
    grad_bias = grad_bias[0].astype(BF16)
    total, *sent = local(
        line_sum_kernel,
        [((tokens, features), F32)] + [((tokens, features), BF16)] * 3,
        got + [share[0]],
        follow=[grad_bias],
    )
    act_mine = placed(activated, act_near, act_far, [total])
    act_other = send(act_mine, OTHER_CORE)
    grad_w_out, done = grad_of((act_mine, act_other), grad_orders, False, [])
    (grad_inputs,) = local(
        last_sum_kernel,
        [((tokens, features), BF16)],
        [send(sent[a - 1], along_first(-STEPS[a])) for a in (3, 2, 1)] + [total],
        follow=[done],
        result=jax.ShapeDtypeStruct,
    )
    return (grad_inputs, grad_w_in, grad_bias, grad_w_out)


def solution(mesh):
    in_specs = (
        P(("col", "dp"), "row"),
        P(("col", "dp"), "row"),
        P("row", ("col", "dp")),
        P(("col", "dp")),
        P(("col", "dp"), "row"),
    )
    out_specs = (
        P(("col", "dp"), "row"),
        P("row", ("col", "dp")),
        P(("col", "dp")),
        P(("col", "dp"), "row"),
    )
    return jax.shard_map(body, mesh=mesh, in_specs=in_specs, out_specs=out_specs, check_vma=False)
```

```python
import functools

import jax
import jax.numpy as jnp
from jax import lax
from jax.experimental import pallas as pl
from jax.experimental.pallas import tpu as pltpu
from jax.sharding import PartitionSpec as P

AXES = ("row", "col", "dp")
Z, CORES, X, Y = 4, 2, 4, 4
BF16, F32 = jnp.bfloat16, jnp.float32
STEPS = (0, 1, 3, 2)
TILE = 256
MIB = 1 << 20
LONG = 60 * 10**9


def place(z, core, x, y):
    return ((z * CORES + core) * 8 + x * 2 + y % 2) * 2 + y // 2


def pairs(source):
    every = [(z, c, x, y) for z in range(Z) for c in range(CORES) for x in range(X) for y in range(Y)]
    return [(place(*source(*at)), place(*at)) for at in every]


def along_first(step):
    return pairs(lambda z, c, x, y: (z, c, x, (y + step) % Y) if c else (z, c, (x + step) % X, y))


def along_second(step):
    return pairs(lambda z, c, x, y: (z, c, (x + step) % X, y) if c else (z, c, x, (y + step) % Y))


Z_ONE = pairs(lambda z, c, x, y: (z ^ (3 if c else 1), c, x, y))
Z_TWO = pairs(lambda z, c, x, y: (z ^ (1 if c else 3), c, x, y))


def along_z(step):
    return pairs(lambda z, c, x, y: ((z + step) % Z, c, x, y))


OTHER_CORE = pairs(lambda z, c, x, y: (z, 1 - c, x, y))


def send(value, perm):
    return lax.ppermute(value, AXES, perm)


def ring(value, along):
    return [send(value, along(STEPS[i])) for i in (3, 2, 1)][::-1]


def local(kernel, outs, args, limit=8, flops=0, follow=(), result=pltpu.VMEM):
    spec = pl.BlockSpec(memory_space=pltpu.VMEM)
    count = len(args)

    def run(*refs):
        kernel(*refs[:count], *refs[count + len(follow) :])

    args = [pltpu.with_memory_space_constraint(a, pltpu.VMEM) for a in args]
    moved = sum(a.size * a.dtype.itemsize for a in args)
    return pl.pallas_call(
        run,
        out_shape=[result(shape, dtype) for shape, dtype in outs],
        in_specs=[spec] * count + [pl.BlockSpec(memory_space=pltpu.HBM if f.size > 2**20 else pl.ANY) for f in follow],
        out_specs=[spec] * len(outs),
        compiler_params=pltpu.CompilerParams(vmem_limit_bytes=limit * MIB),
        cost_estimate=pl.CostEstimate(flops=flops, bytes_accessed=0, transcendentals=0),
    )(*args, *follow)


def at():
    row = lax.axis_index("row")
    z, core = row >> 1, row & 1
    return z, core, z ^ (1 + 2 * core), z ^ (3 - 2 * core)


def span(index, size):
    return pl.ds(pl.multiple_of(index * size, size), size)


def swapped_rows(ref, block, tokens):
    return jnp.concatenate([ref[span(a * 4 + block, tokens), :] for a in range(4)], axis=0)


def stack_kernel(first, second, out, done):
    copies = [pltpu.make_async_copy(ref, out.at[i], done.at[i]) for i, ref in enumerate((first, second))]
    for copy in copies:
        copy.start()
    for copy in copies:
        copy.wait()


def stacked(first, second):
    return pl.pallas_call(
        stack_kernel,
        out_shape=pltpu.VMEM((2,) + first.shape, first.dtype),
        in_specs=[pl.BlockSpec(memory_space=pltpu.HBM)] * 2,
        out_specs=pl.BlockSpec(memory_space=pltpu.VMEM),
        scratch_shapes=[pltpu.SemaphoreType.DMA((2,))],
        compiler_params=pltpu.CompilerParams(vmem_limit_bytes=48 * MIB),
    )(first, second)


def line_kernel(last, far, near, mine, ins, grads):
    tokens = mine.shape[1]
    for i, ref in enumerate((mine, near, far, last)):
        ins[i * tokens : (i + 1) * tokens, :] = ref[0]
        grads[i * tokens : (i + 1) * tokens, :] = ref[1]


def mark_kernel(out):
    out[...] = jnp.zeros_like(out)


def product_kernel(transposed, halves, d, c, b, a, weight, *outs):
    core = lax.axis_index("row") & 1
    rows = jnp.concatenate([a[...], b[...], c[...], d[...]], axis=0)
    for half, out in zip(halves, outs):
        tiles = out.shape[1] // TILE
        for n in range(tiles):
            part = span((core ^ half) * tiles + n, TILE)
            if transposed:
                value = lax.dot_general(
                    rows, weight[part, :], (((1,), (1,)), ((), ())), preferred_element_type=F32
                )
            else:
                value = jnp.dot(rows, weight[:, part], preferred_element_type=F32)
            out[:, n * TILE : (n + 1) * TILE] = value.astype(out.dtype)


def first_sum_kernel(keep, got, sent, mine, near):
    z, _, one, two = at()
    size = mine.shape[0]

    def block(index):
        return keep[span(index, size), :] + swapped_rows(got, index, size // 4).astype(F32)

    sent[0] = block(one).astype(BF16)
    sent[1] = block(z ^ 2).astype(BF16)
    near[...] = block(two)
    mine[...] = block(z)


def second_sum_kernel(mine, near, got, sent, out):
    sent[...] = (near[...] + got[1].astype(F32)).astype(BF16)
    out[...] = mine[...] + got[0].astype(F32)


def gelu_parts(value):
    scale = 0.7978845608028654
    inner = jnp.tanh(scale * (value + 0.044715 * value * value * value))
    slope = 0.5 * (1.0 + inner) + 0.5 * value * (1.0 - inner * inner) * (
        scale * (1.0 + 3.0 * 0.044715 * value * value)
    )
    return 0.5 * value * (1.0 + inner), slope


def activate_kernel(mine, got, bias, activated, slope):
    core = lax.axis_index("row") & 1
    value = mine[...] + got[...].astype(F32) + bias[:, span(core, mine.shape[1])]
    result, derivative = gelu_parts(value)
    activated[...] = result.astype(BF16)
    slope[...] = derivative


def pre_grad_kernel(mine, got, slope, out):
    out[...] = ((mine[...] + got[...].astype(F32)) * slope[...]).astype(BF16)


def pair_kernel(own, near, out):
    out[0] = own[...]
    out[1] = near[...]


def place_ring_kernel(two, three, one, own, out):
    z, size = at()[0], own.shape[0]
    for step, ref in enumerate((own, one, two, three)):
        out[span((z + step) & 3, size), :] = ref[...]


def copy_kernel(value, out):
    out[...] = value[...]


def place_kernel(own, near, far, out):
    z, _, one, two = at()
    size = own.shape[0]
    out[span(z, size), :] = own[...]
    out[span(one, size), :] = near[...]
    out[span(two, size), :] = far[0]
    out[span(z ^ 2, size), :] = far[1]


def orders_kernel(d, c, b, a, own, other):
    size = a.shape[0]
    tokens = size // 4
    for i, slab in enumerate((a, b, c, d)):
        own[i * size : (i + 1) * size, :] = slab[...]
        for k in range(4):
            other[k * size + i * tokens : k * size + (i + 1) * tokens, :] = slab[k * tokens : (k + 1) * tokens, :]


def share_own_kernel(mine, weight, out):
    core = lax.axis_index("row") & 1
    for n in range(out.shape[1] // TILE):
        tile = slice(n * TILE, (n + 1) * TILE)
        out[:, tile] = lax.dot_general(
            mine[...],
            weight[tile, span(core, mine.shape[1])],
            (((1,), (1,)), ((), ())),
            preferred_element_type=F32,
        )


def share_other_kernel(partial, other, weight, *outs):
    core = lax.axis_index("row") & 1
    size = outs[0].shape[0]
    rows = jnp.concatenate([swapped_rows(other, b, size // 4) for b in range(4)], axis=0)
    for n in range(partial.shape[1] // TILE):
        tile = slice(n * TILE, (n + 1) * TILE)
        value = partial[:, tile] + lax.dot_general(
            rows,
            weight[tile, span(1 - core, other.shape[1])],
            (((1,), (1,)), ((), ())),
            preferred_element_type=F32,
        )
        for b, out in enumerate(outs):
            out[:, tile] = value[b * size : (b + 1) * size].astype(out.dtype)


def line_sum_kernel(three, two, one, own, total, *sent):
    value = own[...] + one[...].astype(F32) + two[...].astype(F32) + three[...].astype(F32)
    tokens = total.shape[0]
    total[...] = value[:tokens]
    for i, out in enumerate(sent, 1):
        out[...] = value[i * tokens : (i + 1) * tokens].astype(BF16)


def last_sum_kernel(three, two, one, own, out):
    value = own[...] + one[...].astype(F32) + two[...].astype(F32) + three[...].astype(F32)
    out[...] = value.astype(BF16)


def fetch_kernel(source, follow, out, done):
    del follow
    copy = pltpu.make_async_copy(source, out, done)
    copy.start()
    copy.wait()


def fetch(weight, follow):
    return pl.pallas_call(
        fetch_kernel,
        out_shape=pltpu.VMEM(weight.shape, weight.dtype),
        in_specs=[pl.BlockSpec(memory_space=pltpu.HBM), pl.BlockSpec(memory_space=pl.ANY)],
        out_specs=pl.BlockSpec(memory_space=pltpu.VMEM),
        scratch_shapes=[pltpu.SemaphoreType.DMA],
        compiler_params=pltpu.CompilerParams(vmem_limit_bytes=MIB),
        cost_estimate=pl.CostEstimate(flops=0, bytes_accessed=0, transcendentals=0),
    )(weight, follow)


def grad_kernel(to_columns, left_own, left_other, right_own, right_other, *refs):
    out, total, tiles, sems = refs[-4:]
    core = lax.axis_index("row") & 1
    copies = []
    for i, (left, right) in enumerate(((left_own, right_own), (left_other, right_other))):
        half = core ^ i
        if to_columns:
            size = right.shape[1]
            total[:, span(half, size)] = jnp.sum(right[...].astype(F32), axis=0, keepdims=True)
        else:
            size = left.shape[1]
            total[...] = jnp.zeros_like(total)
        parts = tiles.shape[0] // 2
        width = tiles.shape[2]
        for n in range(parts):
            slot = i * parts + n
            part = slice(n * width, (n + 1) * width)
            tiles[slot] = lax.dot_general(
                left[...], right[:, part], (((0,), (0,)), ((), ())), preferred_element_type=F32
            ).astype(BF16)
            if to_columns:
                target = out.at[:, span(half * parts + n, width)]
            else:
                target = out.at[span(half, size), part]
            copies.append(pltpu.make_async_copy(tiles.at[slot], target, sems.at[slot]))
            copies[-1].start()
    for copy in copies:
        copy.wait()


def grad_of(left, right, to_columns, follow):
    every, rows = left[0].shape
    columns = right[0].shape[1]
    shape = (rows, 2 * columns) if to_columns else (2 * rows, columns)
    width = columns // (2 if to_columns else 3)
    parts = 2 * columns // width
    spec, whole = pl.BlockSpec(memory_space=pltpu.VMEM), pl.BlockSpec(memory_space=pltpu.HBM)
    args = [pltpu.with_memory_space_constraint(a, pltpu.VMEM) for a in [*left, *right]]
    return pl.pallas_call(
        functools.partial(grad_kernel, to_columns),
        out_shape=[jax.ShapeDtypeStruct(shape, BF16), pltpu.VMEM((1, shape[1]), F32)],
        in_specs=[spec] * 4 + [pl.BlockSpec(memory_space=pl.ANY)] * len(follow),
        out_specs=[whole, spec],
        scratch_shapes=[pltpu.VMEM((parts, rows, width), BF16), pltpu.SemaphoreType.DMA((parts,))],
        compiler_params=pltpu.CompilerParams(vmem_limit_bytes=20 * MIB),
        cost_estimate=pl.CostEstimate(flops=0, bytes_accessed=0, transcendentals=0),
    )(*args, *follow)


def both_orders(slabs):
    whole = ((4 * slabs[0].shape[0], slabs[0].shape[1]), BF16)
    return local(orders_kernel, [whole] * 2, slabs[::-1])


def body(inputs, out_grad, w_in, bias_in, w_out):
    tokens, features = inputs.shape
    hidden = w_in.shape[1]
    half, every, line = hidden // 2, 16 * tokens, 4 * tokens

    mine = stacked(inputs, out_grad)
    steps = ring(mine, along_first)
    ins, grads = local(line_kernel, [((line, features), BF16)] * 2, steps[::-1] + [mine])
    ins = [ins] + ring(ins, along_second)
    grads = [grads] + ring(grads, along_second)

    w_in = fetch(w_in, ins[0])
    give, keep = ((every, half), BF16), ((every, half), F32)
    pre_give, pre_keep = local(
        functools.partial(product_kernel, False, (1, 0)), [give, keep], ins[::-1] + [w_in], 16, 0
    )
    quarter = (every // Z, half)

    def first_sum(given, kept, follow=()):
        sent, own, near = local(
            first_sum_kernel,
            [((2,) + quarter, BF16), (quarter, F32), (quarter, F32)],
            [kept, send(given, OTHER_CORE)],
            follow=follow,
        )
        return sent, [own, near, send(sent, Z_ONE)]

    (arrived,) = local(mark_kernel, [((8, 128), F32)], [], flops=LONG, follow=grads[1:])
    pre_sent, pre_sums = first_sum(pre_give, pre_keep, [arrived])
    (act_give,) = local(
        functools.partial(product_kernel, True, (1,)), [give], grads[::-1] + [w_out], 16, 0, [pre_sent]
    )
    (act_keep,) = local(
        functools.partial(product_kernel, True, (0,)), [keep], grads[::-1] + [w_out], 16, 0
    )
    act_sums = first_sum(act_give, act_keep)[1]
    in_orders = both_orders(ins)
    grad_orders = both_orders(grads)
    last = [(quarter, BF16), (quarter, F32)]
    pre_last, pre = local(second_sum_kernel, last, pre_sums, flops=LONG)
    activated, slope = local(
        activate_kernel, last, [pre, send(pre_last, Z_TWO), bias_in[None, :]], flops=LONG
    )
    act_last, act = local(
        second_sum_kernel, last, act_sums, follow=in_orders[:1] + grad_orders[:1]
    )
    (pre_grad,) = local(pre_grad_kernel, last[:1], [act, send(act_last, Z_TWO), slope])

    def paired(value, near, follow=()):
        return local(pair_kernel, [((2,) + quarter, BF16)], [value, near], follow=follow)[0]

    def placed(value, near, far, follow=()):
        return local(place_kernel, [((every, half), BF16)], [value, near, far], follow=follow)[0]

    def gathered(value, follow):
        return local(
            place_ring_kernel, [((every, half), BF16)], [send(value, along_z(d)) for d in (2, 3, 1)] + [value], follow=follow
        )[0]

    act_near = send(activated, Z_ONE)
    act_far = send(paired(activated, act_near), Z_TWO)
    pg_mine = gathered(pre_grad, [act_near])
    pg_other = send(pg_mine, OTHER_CORE)
    (partial,) = local(share_own_kernel, [((every, features), F32)], [pg_mine, w_in], 16, 0)
    share = local(
        share_other_kernel,
        [((line, features), F32)] + [((line, features), BF16)] * 3,
        [partial, pg_other, w_in],
        16,
        0,
    )
    got = [send(share[b], along_second(-STEPS[b])) for b in (3, 2, 1)]

    grad_w_in, grad_bias = grad_of(in_orders, (pg_mine, pg_other), True, [share[1]])
    grad_bias = grad_bias[0].astype(BF16)
    total, *sent = local(
        line_sum_kernel,
        [((tokens, features), F32)] + [((tokens, features), BF16)] * 3,
        got + [share[0]],
        follow=[grad_bias],
    )
    act_mine = placed(activated, act_near, act_far, [total])
    act_other = send(act_mine, OTHER_CORE)
    grad_w_out, done = grad_of((act_mine, act_other), grad_orders, False, [])
    (grad_inputs,) = local(
        last_sum_kernel,
        [((tokens, features), BF16)],
        [send(sent[a - 1], along_first(-STEPS[a])) for a in (3, 2, 1)] + [total],
        follow=[done],
        result=jax.ShapeDtypeStruct,
    )
    return (grad_inputs, grad_w_in, grad_bias, grad_w_out)


def solution(mesh):
    in_specs = (
        P(("col", "dp"), "row"),
        P(("col", "dp"), "row"),
        P("row", ("col", "dp")),
        P(("col", "dp")),
        P(("col", "dp"), "row"),
    )
    out_specs = (
        P(("col", "dp"), "row"),
        P("row", ("col", "dp")),
        P(("col", "dp")),
        P(("col", "dp"), "row"),
    )
    return jax.shard_map(body, mesh=mesh, in_specs=in_specs, out_specs=out_specs, check_vma=False)
```
